32 devices in a mesh: groups: 2 (over y), outer: 4 (over z), bulk: 2 (over x), inner: 2 (over core).
Axes of the slice: x: 2, y: 2, z: 4, core: 2. Of those that a mesh axis runs over, the one named last changes fastest.
Arguments:
- points: bfloat16 [2048, 1152], P(('groups', 'outer', 'bulk', 'inner')), parts along dimension 0, may hold values from -17 to 17
- coarse_ids: int32 [2048, 8], P(('groups', 'outer', 'bulk', 'inner')), parts along dimension 0, may hold values from 0 to 511, as said below
- fine_cent: bfloat16 [1024, 128, 1152], P(('groups', 'outer', 'bulk', 'inner')), parts along dimension 0, may hold values from -6 to 6
- slot_live: int32 [1024, 128], P(('groups', 'outer', 'bulk', 'inner')), parts along dimension 0, may hold values from 0 to 1, as said below
- coarse_cent: bfloat16 [1024, 1152], P(('groups', 'outer', 'bulk', 'inner')), parts along dimension 0, may hold values from -6 to 6
Outputs:
- fine_out: bfloat16 [1024, 128, 1152], P(('groups', 'outer', 'bulk', 'inner')), parts along dimension 0
- coarse_out: bfloat16 [1024, 1152], P(('groups', 'outer', 'bulk', 'inner')), parts along dimension 0
The draws below stay inside these ranges and needn't reach their ends.
There are 2 independent parts, one for each index of `groups`. The reference program is written for one: setup_inputs(seed, part) draws one part's arguments, and reference() takes and returns one part's arrays. A program takes and returns all parts, laid end to end along the dimension named above; each array names one. Nothing has to cross between parts.
Inputs may be any that keep to these rules, and one draw needn't show every extreme that they name: `coarse_ids`: each row names 8 different coarse clusters. Within the rows of one device no coarse cluster is named by more than 2 rows, and on every device some clusters are named by exactly 2 rows. `slot_live`: slots 0 and 1 of every block are live.
All inputs are finite; a program needn't handle non-finite values.
Results may differ from the reference program's by a relative error of at most 0.0055.
Values may be sent and summed in bfloat16 or wider, within the bound.
A program may use at most 128 MiB of HBM per device.

```python
import math
import jax
import jax.numpy as jnp
from jax import lax

D = 1152
KC = 512
BS = 128
TOP = 8
MOST = 2
ITERS = 2
PTS_DEV = 64
POINTS = 1024
N_OUTER = 4
N_BULK = 2
N_INNER = 2


def fine_normals(key):
    return jnp.clip(jax.random.normal(key, (KC, BS, D), jnp.float32), -6.0, 6.0)


def route_table(key):
    global_order = jax.random.permutation(jax.random.fold_in(key, 101), KC).astype(jnp.int32)
    device_count = POINTS // PTS_DEV
    hot_count = PTS_DEV * TOP // (4 * MOST)
    rest_count = MOST // 2

    def one_block(block_key):
        shuffle = jax.random.permutation(jax.random.fold_in(block_key, 1), KC - hot_count).astype(jnp.int32)
        cluster_order = jnp.concatenate([global_order[:hot_count], global_order[hot_count:][shuffle]])
        position = jnp.arange(PTS_DEV * TOP, dtype=jnp.int32)
        rank_of = jnp.where(position < hot_count * MOST, position // MOST, hot_count + (position - hot_count * MOST) // rest_count)
        sequence = cluster_order[rank_of]
        table = sequence.reshape(TOP, PTS_DEV).T
        column_keys = jax.random.split(jax.random.fold_in(block_key, 3), PTS_DEV)
        column_order = jax.vmap(lambda row_key: jax.random.permutation(row_key, TOP).astype(jnp.int32))(column_keys)
        table = jnp.take_along_axis(table, column_order, axis=1)
        row_order = jax.random.permutation(jax.random.fold_in(block_key, 2), PTS_DEV).astype(jnp.int32)
        return table[row_order]
    block_keys = jax.random.split(jax.random.fold_in(key, 102), device_count)
    return jax.vmap(one_block)(block_keys).reshape(POINTS, TOP).astype(jnp.int32)


def draw_coarse_ids(key, part):
    return route_table(key)


def draw_fine_cent(key, part):
    normals = fine_normals(key)
    return normals.astype(jnp.bfloat16)


def draw_slot_live(key, part):
    key = jax.random.fold_in(key, 9)
    coins = jax.random.randint(key, (KC, BS), 0, 4)
    slot_number = jnp.arange(BS, dtype=jnp.int32)[None, :]
    return jnp.where((coins != 0) | (slot_number < 2), 1, 0).astype(jnp.int32)


def draw_points(key, part):
    key = jax.random.fold_in(key, 7)
    values = jnp.clip(jax.random.normal(key, (POINTS, D), jnp.float32), -6.0, 6.0)
    return values.astype(jnp.bfloat16)


def block_levels(stream_key, dims, shards, smallest, high):
    def one(dim, shards_of):
        heights = jax.random.uniform(jax.random.fold_in(jax.random.fold_in(stream_key, 6), dim), (shards_of,), jnp.float32, smallest / len(shards), high / len(shards))
        return jnp.repeat(jnp.exp(heights), dims[dim] // shards_of).reshape((-1,) + (1,) * (len(dims) - dim - 1))

    gain = one(*shards[0])
    for cut in shards[1:]:
        gain = gain * one(*cut)
    return gain


def gaussian(key, extent, width, limit, cuts=(), kind=jnp.bfloat16):
    entries = jax.random.normal(key, extent, jnp.float32) * width
    if len(cuts) > 0:
        entries = block_levels(key, extent, cuts, -0.22, 0.18) * entries
    return jnp.clip(entries, min=-limit, max=limit).astype(kind)


def setup_inputs(seed: int = 0, part: int = 0) -> dict:
    keys = jax.random.split(jax.random.key(seed), 6)
    own_keys = jax.random.split(jax.random.fold_in(keys[5], part), 6)
    return {
        "points": draw_points(jax.random.fold_in(jax.random.fold_in(keys[5], part), 71), part),
        "coarse_ids": draw_coarse_ids(jax.random.fold_in(jax.random.fold_in(keys[5], part), 71), part),
        "fine_cent": draw_fine_cent(jax.random.fold_in(jax.random.fold_in(keys[5], part), 71), part),
        "slot_live": draw_slot_live(jax.random.fold_in(jax.random.fold_in(keys[5], part), 71), part),
        "coarse_cent": gaussian(own_keys[4], (KC, D), 1.0, 6.0, ((0, 16),)),
    }


PRIOR = 1.0

def reference(points, coarse_ids, fine_cent, slot_live, coarse_cent):
    owner_count = N_OUTER * N_BULK * N_INNER
    capacity = MOST * owner_count
    pair_total = POINTS * TOP
    pair_ids = coarse_ids.reshape(pair_total).astype(jnp.int32)
    ordering = jnp.argsort(pair_ids, stable=True).astype(jnp.int32)
    counts = jnp.zeros((KC,), jnp.int32).at[pair_ids].add(1)
    starts = (jnp.cumsum(counts) - counts).astype(jnp.int32)
    padded = jnp.concatenate([ordering, jnp.full((capacity,), pair_total, jnp.int32)])
    members = lax.map(lambda cluster: lax.dynamic_slice(padded, (starts[cluster],), (capacity,)), jnp.arange(KC, dtype=jnp.int32))
    valid = jnp.arange(capacity, dtype=jnp.int32)[None, :] < counts[:, None]
    members = jnp.where(valid, members, pair_total).astype(jnp.int32)
    member_point = (jnp.minimum(members, pair_total - 1) // TOP).astype(jnp.int32)
    live_mask = slot_live == 1
    inv_root = 1.0 / math.sqrt(D)
    fine_now = fine_cent
    coarse_now = coarse_cent
    for step_index in range(ITERS):

        def logits_of(cluster, fine_now=fine_now, coarse_now=coarse_now):
            rows = points[member_point[cluster]].astype(jnp.float32)
            fine_wide = fine_now[cluster].astype(jnp.float32)
            coarse_wide = coarse_now[cluster].astype(jnp.float32)
            products = jnp.dot(rows, fine_wide.T, preferred_element_type=jnp.float32)
            half_fine = 0.5 * lax.optimization_barrier(jnp.sum(fine_wide * fine_wide, axis=-1))
            coarse_term = (jnp.dot(rows, coarse_wide, preferred_element_type=jnp.float32) - 0.5 * jnp.sum(coarse_wide * coarse_wide)) * inv_root
            logits = (products - half_fine[None, :]) * inv_root + coarse_term[:, None]
            return (jnp.where(live_mask[cluster][None, :], logits, -jnp.inf), rows, fine_wide)

        def block_stats(cluster):
            masked, rows, fine_wide = logits_of(cluster)
            block_max = lax.optimization_barrier(jnp.max(masked, axis=-1))
            block_sum = lax.optimization_barrier(jnp.sum(jnp.exp(masked - block_max[:, None]), axis=-1))
            return (block_max, block_sum)
        block_max, block_sum = lax.map(block_stats, jnp.arange(KC, dtype=jnp.int32))
        flat_members = members.reshape(KC * capacity)
        pair_max = jnp.zeros((pair_total,), jnp.float32).at[flat_members].set(block_max.reshape(KC * capacity), mode='drop')
        pair_sum = jnp.zeros((pair_total,), jnp.float32).at[flat_members].set(block_sum.reshape(KC * capacity), mode='drop')
        grid_max = pair_max.reshape(POINTS, TOP)
        point_max = lax.optimization_barrier(jnp.max(grid_max, axis=1))
        point_sum = lax.optimization_barrier(jnp.sum(pair_sum.reshape(POINTS, TOP) * jnp.exp(grid_max - point_max[:, None]), axis=1))
        point_inv = 1.0 / point_sum
        member_shift = point_max[member_point]
        member_inv = jnp.where(valid, point_inv[member_point], 0.0)

        def refresh(cluster):
            masked, rows, fine_wide = logits_of(cluster)
            weights = (jnp.exp(masked - member_shift[cluster][:, None]) * member_inv[cluster][:, None]).astype(jnp.bfloat16)
            weights_wide = weights.astype(jnp.float32)
            mass = PRIOR + lax.optimization_barrier(jnp.sum(weights_wide, axis=0))
            totals = PRIOR * fine_wide + jnp.dot(weights_wide.T, rows, preferred_element_type=jnp.float32)
            fine_new = jnp.where(live_mask[cluster][:, None], totals / mass[:, None], fine_wide).astype(jnp.bfloat16)
            live_mass = jnp.where(live_mask[cluster], mass, 0.0)
            coarse_new = (jnp.dot(live_mass, fine_new.astype(jnp.float32), precision=lax.Precision.HIGHEST) / jnp.sum(live_mass)).astype(jnp.bfloat16)
            return (fine_new, coarse_new)
        fine_now, coarse_now = lax.map(refresh, jnp.arange(KC, dtype=jnp.int32))
    return (fine_now, coarse_now)
```

```python
import functools
import math

import jax
import jax.numpy as jnp
from jax import lax
from jax.experimental import pallas as pl
from jax.experimental.pallas import tpu as pltpu
from jax.sharding import PartitionSpec as P

MOST = 2
ITERS = 2
PRIOR = 1.0
LOW = -3.0e38
AXES = ("outer", "bulk", "inner")
VMEM = 56 * 1024 * 1024


def pick_kernel(seg, ids_ref, x_ref, key_ref, xs_ref):
    blocks, lanes = key_ref.shape
    rows = xs_ref.shape[2]
    block = lax.broadcasted_iota(jnp.int32, (blocks, lanes), 0)
    pos = lax.broadcasted_iota(jnp.int32, (blocks, lanes), 1)
    member = jnp.zeros((blocks, lanes), jnp.int32)
    for k in range(ids_ref.shape[0]):
        member = jnp.where(ids_ref[k : k + 1, :] == block, 1, member)
    count = member
    inside = lax.rem(pos, seg)
    shift = 1
    while shift < seg:
        count = count + jnp.where(inside >= shift, pltpu.roll(count, shift, 1), 0)
        shift *= 2
    key = jnp.where(member == 1, (pos // seg) * MOST + count - member, -1)
    key_ref[...] = key
    row = lax.broadcasted_iota(jnp.int32, (rows, lanes), 0)
    group = max(1, min(blocks, 256 // rows))
    for g in range(0, blocks, group):
        hot = jnp.concatenate(
            [jnp.where(key[b : b + 1, :] == row, 1.0, 0.0) for b in range(g, g + group)], axis=0
        ).astype(jnp.bfloat16)
        got = jnp.dot(hot, x_ref[...], preferred_element_type=jnp.float32)
        xs_ref[0, g : g + group] = got.astype(jnp.bfloat16).reshape(group, rows, got.shape[1])


def lane_sum(x):
    total = x[:, :128]
    for j in range(128, x.shape[1], 128):
        total = total + x[:, j : j + 128]
    return total


def column(row):
    return jnp.broadcast_to(row, (128, 128)).T


def stats(fine, coarse, live, b, first, inv_root, key_ref, xs_ref, logit_ref, m_scr, s_scr, i):
    chunks, _, rows, _ = xs_ref.shape
    wide = fine.astype(jnp.float32)
    half = 0.5 * jnp.sum(lane_sum(wide * wide).T, axis=0, keepdims=True)
    cw = coarse.astype(jnp.float32)
    half_c = 0.5 * jnp.sum(cw * cw, axis=1, keepdims=True)
    lanes = key_ref.shape[1] // chunks
    row = lax.broadcasted_iota(jnp.int32, (rows, lanes), 0)
    for c in range(chunks):
        x = xs_ref[c, b]
        prod = lax.dot_general(
            x, fine, (((1,), (1,)), ((), ())), preferred_element_type=jnp.float32
        )
        shift = jnp.sum(lane_sum(x.astype(jnp.float32) * cw), axis=1, keepdims=True)
        logit = (prod - half) * inv_root + (shift - half_c) * inv_root
        logit = jnp.where(live == 1, logit, -jnp.inf)
        logit_ref[c, b] = logit
        m = jnp.max(logit, axis=1, keepdims=True)
        s = jnp.sum(jnp.exp(logit - m), axis=1, keepdims=True)
        part = pl.ds(c * lanes, lanes)
        hot = key_ref[b : b + 1, part] == row
        m_scr[i, b : b + 1, part] = jnp.sum(jnp.where(hot, m, 0.0), axis=0, keepdims=True)
        s_scr[i, b : b + 1, part] = jnp.sum(jnp.where(hot, s, 0.0), axis=0, keepdims=True)


def finish(keys_ref, m_scr, s_scr, stat_ref):
    steps, per, _ = m_scr.shape
    top = jnp.full((1, m_scr.shape[2]), LOW, jnp.float32)
    for i in range(steps):
        has = keys_ref[i] >= 0
        top = jnp.maximum(top, jnp.max(jnp.where(has, m_scr[i], LOW), axis=0, keepdims=True))
    total = jnp.zeros_like(top)
    for i in range(steps):
        has = keys_ref[i] >= 0
        term = s_scr[i] * jnp.exp(jnp.where(has, m_scr[i], LOW) - top)
        total = total + jnp.sum(jnp.where(has, term, 0.0), axis=0, keepdims=True)
    stat_ref[0:1, :] = top
    stat_ref[1:2, :] = total


def combine(all_ref, point_scr):
    top = all_ref[0, 0:1, :]
    for n in range(1, all_ref.shape[0]):
        top = jnp.maximum(top, all_ref[n, 0:1, :])
    total = jnp.zeros_like(top)
    for n in range(all_ref.shape[0]):
        total = total + all_ref[n, 1:2, :] * jnp.exp(all_ref[n, 0:1, :] - top)
    point_scr[0:1, :] = top
    point_scr[1:2, :] = 1.0 / total


def refresh(fine, live, b, key_ref, xs_ref, logit_ref, point_scr):
    chunks, _, rows, _ = xs_ref.shape
    lanes = key_ref.shape[1] // chunks
    row = lax.broadcasted_iota(jnp.int32, (rows, lanes), 0)
    mass = jnp.full((1, 128), PRIOR, jnp.float32)
    total = PRIOR * fine.astype(jnp.float32)
    for c in range(chunks):
        part = pl.ds(c * lanes, lanes)
        hot = key_ref[b : b + 1, part] == row
        top = jnp.sum(jnp.where(hot, point_scr[0:1, part], 0.0), axis=1, keepdims=True)
        inv = jnp.sum(jnp.where(hot, point_scr[1:2, part], 0.0), axis=1, keepdims=True)
        top = jnp.where(inv > 0.0, top, -LOW)
        w = (jnp.exp(logit_ref[c, b] - top) * inv).astype(jnp.bfloat16)
        mass = mass + jnp.sum(w.astype(jnp.float32), axis=0, keepdims=True)
        total = total + lax.dot_general(
            w, xs_ref[c, b], (((0,), (0,)), ((), ())), preferred_element_type=jnp.float32
        )
    recip = column(1.0 / mass)
    live_mass = jnp.where(live == 1, mass, 0.0)
    share = column(live_mass)
    news, sums = [], []
    for j in range(0, fine.shape[1], 128):
        new = (total[:, j : j + 128] * recip).astype(jnp.bfloat16)
        news.append(new)
        sums.append(jnp.sum(new.astype(jnp.float32) * share, axis=0, keepdims=True))
    coarse = jnp.concatenate(sums, axis=1) / jnp.sum(live_mass, axis=1, keepdims=True)
    return jnp.concatenate(news, axis=1), coarse.astype(jnp.bfloat16)


def first_kernel(inv_root, fine_ref, coarse_ref, live_ref, key_ref, keys_ref, xs_ref,
                 logit_ref, stat_ref, m_scr, s_scr):
    i = pl.program_id(0)
    for b in range(fine_ref.shape[0]):
        stats(fine_ref[b], coarse_ref[0, b : b + 1, :], live_ref[0, b : b + 1, :], b, 0, inv_root,
              key_ref.at[0], xs_ref, logit_ref, m_scr, s_scr, i)

    @pl.when(i == pl.num_programs(0) - 1)
    def _():
        finish(keys_ref, m_scr, s_scr, stat_ref)


def middle_kernel(inv_root, fine_ref, live_ref, key_ref, keys_ref, xs_ref, logit_ref, all_ref,
                  new_ref, out_logit_ref, stat_ref, m_scr, s_scr, point_scr):
    i = pl.program_id(0)

    @pl.when(i == 0)
    def _():
        combine(all_ref, point_scr)

    for b in range(fine_ref.shape[0]):
        live = live_ref[0, b : b + 1, :]
        fine, coarse = refresh(fine_ref[b], live, b, key_ref.at[0], xs_ref, logit_ref, point_scr)
        new_ref[b] = fine
        stats(fine, coarse, live, b, 0, inv_root, key_ref.at[0], xs_ref, out_logit_ref, m_scr,
              s_scr, i)

    @pl.when(i == pl.num_programs(0) - 1)
    def _():
        finish(keys_ref, m_scr, s_scr, stat_ref)


def last_kernel(fine_ref, live_ref, key_ref, xs_ref, logit_ref, all_ref, new_ref, coarse_ref,
                point_scr):
    i = pl.program_id(0)

    @pl.when(i == 0)
    def _():
        combine(all_ref, point_scr)

    for b in range(fine_ref.shape[0]):
        live = live_ref[0, b : b + 1, :]
        fine, coarse = refresh(fine_ref[b], live, b, key_ref.at[0], xs_ref, logit_ref, point_scr)
        new_ref[b] = fine
        coarse_ref[0, b : b + 1, :] = coarse


def spread_points(x):
    return lax.all_gather(x, AXES, axis=0, tiled=True)


def spread_stats(stat):
    return lax.all_gather(stat, AXES, axis=0, tiled=False)


def shards(points, coarse_ids, fine_cent, slot_live, coarse_cent):
    seg, top_count = coarse_ids.shape
    blocks, slots, feature = fine_cent.shape
    owners = lax.axis_size(AXES)
    me = lax.axis_index(AXES)
    total = owners * seg
    senders = min(owners, 16)
    chunks = owners // senders
    lanes = senders * seg
    rows = senders * MOST
    inv_root = 1.0 / math.sqrt(feature)
    per = min(blocks, 4)
    steps = blocks // per
    f32, bf16 = jnp.float32, jnp.bfloat16
    params = pltpu.CompilerParams(vmem_limit_bytes=VMEM, dimension_semantics=("arbitrary",))

    all_ids = lax.all_gather(coarse_ids, AXES, axis=0, tiled=True)
    rel_ids = all_ids.T - me * blocks
    all_points = spread_points(points)

    key, xs = pl.pallas_call(
        functools.partial(pick_kernel, seg),
        grid=(chunks,),
        in_specs=[
            pl.BlockSpec((top_count, lanes), lambda i: (0, i)),
            pl.BlockSpec((lanes, feature), lambda i: (i, 0)),
        ],
        out_specs=[
            pl.BlockSpec((blocks, lanes), lambda i: (0, i)),
            pl.BlockSpec((1, blocks, rows, feature), lambda i: (i, 0, 0, 0)),
        ],
        out_shape=[
            jax.ShapeDtypeStruct((blocks, total), jnp.int32),
            jax.ShapeDtypeStruct((chunks, blocks, rows, feature), bf16),
        ],
        compiler_params=params,
        name="pick",
    )(rel_ids, all_points)

    keys = key.reshape(steps, per, total)
    live = slot_live.reshape(steps, per, slots)
    coarse = coarse_cent.reshape(steps, per, feature)

    fine_spec = pl.BlockSpec((per, slots, feature), lambda i: (i, 0, 0))
    coarse_spec = pl.BlockSpec((1, per, feature), lambda i: (i, 0, 0))
    live_spec = pl.BlockSpec((1, per, slots), lambda i: (i, 0, 0))
    key_spec = pl.BlockSpec((1, per, total), lambda i: (i, 0, 0))
    keys_spec = pl.BlockSpec((steps, per, total), lambda i: (0, 0, 0))
    xs_spec = pl.BlockSpec((chunks, per, rows, feature), lambda i: (0, i, 0, 0))
    logit_spec = pl.BlockSpec((chunks, per, rows, slots), lambda i: (0, i, 0, 0))
    stat_spec = pl.BlockSpec((2, total), lambda i: (0, 0))
    all_spec = pl.BlockSpec((owners, 2, total), lambda i: (0, 0, 0))
    fine_shape = jax.ShapeDtypeStruct((blocks, slots, feature), bf16)
    logit_shape = jax.ShapeDtypeStruct((chunks, blocks, rows, slots), f32)
    stat_shape = jax.ShapeDtypeStruct((2, total), f32)
    grid_scr = pltpu.VMEM((steps, per, total), f32)
    point_scr = pltpu.VMEM((2, total), f32)

    logit, stat = pl.pallas_call(
        functools.partial(first_kernel, inv_root),
        grid=(steps,),
        in_specs=[fine_spec, coarse_spec, live_spec, key_spec, keys_spec, xs_spec],
        out_specs=[logit_spec, stat_spec],
        out_shape=[logit_shape, stat_shape],
        scratch_shapes=[grid_scr, grid_scr],
        compiler_params=params,
        name="first",
    )(fine_cent, coarse, live, keys, keys, xs)
    fine = fine_cent
    for _ in range(ITERS - 1):
        every = spread_stats(stat)
        fine, logit, stat = pl.pallas_call(
            functools.partial(middle_kernel, inv_root),
            grid=(steps,),
            in_specs=[fine_spec, live_spec, key_spec, keys_spec, xs_spec, logit_spec, all_spec],
            out_specs=[fine_spec, logit_spec, stat_spec],
            out_shape=[fine_shape, logit_shape, stat_shape],
            scratch_shapes=[grid_scr, grid_scr, point_scr],
            compiler_params=params,
            name="middle",
        )(fine, live, keys, keys, xs, logit, every)
    every = spread_stats(stat)
    fine, coarse = pl.pallas_call(
        last_kernel,
        grid=(steps,),
        in_specs=[fine_spec, live_spec, key_spec, xs_spec, logit_spec, all_spec],
        out_specs=[fine_spec, coarse_spec],
        out_shape=[fine_shape, jax.ShapeDtypeStruct((steps, per, feature), bf16)],
        scratch_shapes=[point_scr],
        compiler_params=params,
        name="last",
    )(fine, live, keys, xs, logit, every)
    return fine, coarse.reshape(blocks, feature)


def solution(mesh):
    spec = P(("groups",) + AXES)
    return jax.shard_map(
        shards, mesh=mesh, in_specs=(spec,) * 5, out_specs=(spec,) * 2, check_vma=False
    )
```

```python
import functools
import math

import jax
import jax.numpy as jnp
from jax import lax
from jax.experimental import pallas as pl
from jax.experimental.pallas import tpu as pltpu
from jax.sharding import PartitionSpec as P

MOST = 2
ITERS = 2
PRIOR = 1.0
LOW = -3.0e38
AXES = ("outer", "bulk", "inner")
VMEM = 56 * 1024 * 1024


def pick_kernel(seg, ids_ref, x_ref, key_ref, xs_ref):
    blocks, lanes = key_ref.shape
    rows = xs_ref.shape[2]
    block = lax.broadcasted_iota(jnp.int32, (blocks, lanes), 0)
    pos = lax.broadcasted_iota(jnp.int32, (blocks, lanes), 1)
    z, x, c = [lax.axis_index(a) for a in AXES]
    me = (z * lax.axis_size("bulk") + x) * lax.axis_size("inner") + c
    pack = 128 // seg
    part = lax.broadcasted_iota(jnp.int32, ids_ref.shape[1:], 1) // seg
    tiles = []
    for j in range(0, ids_ref.shape[0], pack):
        tile = ids_ref[j]
        for q in range(1, pack):
            tile = jnp.where(part == q, ids_ref[j + q], tile)
        tiles.append(tile)
    ids = jnp.concatenate(tiles, axis=1) - me * blocks
    member = jnp.zeros((blocks, lanes), jnp.int32)
    for k in range(ids.shape[0]):
        member = jnp.where(ids[k : k + 1, :] == block, 1, member)
    count = member
    inside = lax.rem(pos, seg)
    shift = 1
    while shift < seg:
        count = count + jnp.where(inside >= shift, pltpu.roll(count, shift, 1), 0)
        shift *= 2
    key = jnp.where(member == 1, (pos // seg) * MOST + count - member, -1)
    key_ref[...] = key
    row = lax.broadcasted_iota(jnp.int32, (rows, lanes), 0)
    group = max(1, min(blocks, 256 // rows))
    for g in range(0, blocks, group):
        hot = jnp.concatenate(
            [jnp.where(key[b : b + 1, :] == row, 1.0, 0.0) for b in range(g, g + group)], axis=0
        ).astype(jnp.bfloat16)
        got = jnp.dot(hot, x_ref[...], preferred_element_type=jnp.float32)
        xs_ref[0, g : g + group] = got.astype(jnp.bfloat16).reshape(group, rows, got.shape[1])


def lane_sum(x):
    total = x[:, :128]
    for j in range(128, x.shape[1], 128):
        total = total + x[:, j : j + 128]
    return total


def column(row):
    return jnp.broadcast_to(row, (128, 128)).T


def stats(fine, cw, live, b, n, inv_root, key_ref, xs_ref, logit_ref, m_scr, s_scr):
    chunks, _, rows, _ = xs_ref.shape
    wide = fine.astype(jnp.float32)
    half = 0.5 * jnp.sum(lane_sum(wide * wide).T, axis=0, keepdims=True)
    half_c = 0.5 * jnp.sum(cw * cw, axis=1, keepdims=True)
    lanes = key_ref.shape[1] // chunks
    row = lax.broadcasted_iota(jnp.int32, (rows, lanes), 0)
    for c in range(chunks):
        x = xs_ref[c, b]
        prod = lax.dot_general(
            x, fine, (((1,), (1,)), ((), ())), preferred_element_type=jnp.float32
        )
        shift = jnp.sum(lane_sum(x.astype(jnp.float32) * cw), axis=1, keepdims=True)
        logit = (prod - half) * inv_root + (shift - half_c) * inv_root
        logit = jnp.where(live == 1, logit, -jnp.inf)
        logit_ref[c, b] = logit
        m = jnp.max(logit, axis=1, keepdims=True)
        s = jnp.sum(jnp.exp(logit - m), axis=1, keepdims=True)
        part = pl.ds(c * lanes, lanes)
        hot = key_ref[pl.ds(n, 1), part] == row
        m_scr[pl.ds(n, 1), part] = jnp.sum(jnp.where(hot, m, 0.0), axis=0, keepdims=True)
        s_scr[pl.ds(n, 1), part] = jnp.sum(jnp.where(hot, s, 0.0), axis=0, keepdims=True)


def finish(key_ref, m_scr, s_scr, stat_ref):
    has = key_ref[...] >= 0
    large = jnp.where(has, m_scr[...], LOW)
    top = jnp.max(large, axis=0, keepdims=True)
    term = s_scr[...] * jnp.exp(large - top)
    stat_ref[0:1, :] = top
    stat_ref[1:2, :] = jnp.sum(jnp.where(has, term, 0.0), axis=0, keepdims=True)


def combine(all_ref, point_scr):
    top = all_ref[0, 0:1, :]
    for n in range(1, all_ref.shape[0]):
        top = jnp.maximum(top, all_ref[n, 0:1, :])
    total = jnp.zeros_like(top)
    for n in range(all_ref.shape[0]):
        total = total + all_ref[n, 1:2, :] * jnp.exp(all_ref[n, 0:1, :] - top)
    point_scr[0:1, :] = top
    point_scr[1:2, :] = 1.0 / total


def refresh(fine, live, b, n, key_ref, xs_ref, logit_ref, point_scr):
    chunks, _, rows, _ = xs_ref.shape
    lanes = key_ref.shape[1] // chunks
    row = lax.broadcasted_iota(jnp.int32, (rows, lanes), 0)
    mass = jnp.full((1, 128), PRIOR, jnp.float32)
    total = PRIOR * fine.astype(jnp.float32)
    for c in range(chunks):
        part = pl.ds(c * lanes, lanes)
        hot = key_ref[pl.ds(n, 1), part] == row
        top = jnp.sum(jnp.where(hot, point_scr[0:1, part], 0.0), axis=1, keepdims=True)
        inv = jnp.sum(jnp.where(hot, point_scr[1:2, part], 0.0), axis=1, keepdims=True)
        top = jnp.where(inv > 0.0, top, -LOW)
        w = (jnp.exp(logit_ref[c, b] - top) * inv).astype(jnp.bfloat16)
        mass = mass + jnp.sum(w.astype(jnp.float32), axis=0, keepdims=True)
        total = total + lax.dot_general(
            w, xs_ref[c, b], (((0,), (0,)), ((), ())), preferred_element_type=jnp.float32
        )
    recip = column(1.0 / mass)
    live_mass = jnp.where(live == 1, mass, 0.0)
    share = column(live_mass)
    news, sums = [], []
    for j in range(0, fine.shape[1], 128):
        new = (total[:, j : j + 128] * recip).astype(jnp.bfloat16)
        news.append(new)
        sums.append(jnp.sum(new.astype(jnp.float32) * share, axis=0, keepdims=True))
    coarse = jnp.concatenate(sums, axis=1) / jnp.sum(live_mass, axis=1, keepdims=True)
    return jnp.concatenate(news, axis=1), coarse.astype(jnp.bfloat16)


def first_kernel(inv_root, fine_ref, coarse_ref, live_ref, key_ref, xs_ref, logit_ref, stat_ref,
                 m_scr, s_scr, coarse_scr):
    i = pl.program_id(0)
    per = fine_ref.shape[0]

    @pl.when(i == 0)
    def _():
        coarse_scr[...] = coarse_ref[...].astype(jnp.float32)

    for b in range(per):
        n = i * per + b
        stats(fine_ref[b], coarse_scr[pl.ds(n, 1), :], live_ref[pl.ds(n, 1), :], b, n, inv_root,
              key_ref, xs_ref, logit_ref, m_scr, s_scr)

    @pl.when(i == pl.num_programs(0) - 1)
    def _():
        finish(key_ref, m_scr, s_scr, stat_ref)


def middle_kernel(inv_root, fine_ref, live_ref, key_ref, xs_ref, logit_ref, all_ref,
                  new_ref, out_logit_ref, stat_ref, m_scr, s_scr, point_scr):
    i = pl.program_id(0)
    per = fine_ref.shape[0]

    @pl.when(i == 0)
    def _():
        combine(all_ref, point_scr)

    for b in range(per):
        n = i * per + b
        live = live_ref[pl.ds(n, 1), :]
        fine, coarse = refresh(fine_ref[b], live, b, n, key_ref, xs_ref, logit_ref, point_scr)
        new_ref[b] = fine
        stats(fine, coarse.astype(jnp.float32), live, b, n, inv_root, key_ref, xs_ref,
              out_logit_ref, m_scr, s_scr)

    @pl.when(i == pl.num_programs(0) - 1)
    def _():
        finish(key_ref, m_scr, s_scr, stat_ref)


def last_kernel(fine_ref, live_ref, key_ref, xs_ref, logit_ref, all_ref, new_ref, coarse_ref,
                point_scr, coarse_scr):
    i = pl.program_id(0)
    per = fine_ref.shape[0]

    @pl.when(i == 0)
    def _():
        combine(all_ref, point_scr)

    for b in range(per):
        n = i * per + b
        live = live_ref[pl.ds(n, 1), :]
        fine, coarse = refresh(fine_ref[b], live, b, n, key_ref, xs_ref, logit_ref, point_scr)
        new_ref[b] = fine
        coarse_scr[pl.ds(n, 1), :] = coarse.astype(jnp.float32)

    @pl.when(i == pl.num_programs(0) - 1)
    def _():
        coarse_ref[...] = coarse_scr[...].astype(jnp.bfloat16)


MESH = pl.DeviceIdType.MESH


def place():
    _, width, cores = [lax.axis_size(a) for a in AXES]
    group = lax.axis_index("groups")
    z, x, c = [lax.axis_index(a) for a in AXES]

    def device(n):
        return (group, n // (width * cores), lax.rem(n // cores, width), lax.rem(n, cores))

    return (z * width + x) * cores + c, device


def greet(owners, me, device):
    barrier = pltpu.get_barrier_semaphore()

    def hello(d, carry):
        peer = lax.rem(me + d, owners)
        pl.semaphore_signal(barrier, inc=1, device_id=device(peer), device_id_type=MESH)
        return carry

    lax.fori_loop(1, owners, hello, 0)
    pl.semaphore_wait(barrier, owners - 1)


def direct(owners, me, device, src, dst, send_sem, recv_sem):
    def copy(peer, slot):
        return pltpu.make_async_remote_copy(
            src_ref=src, dst_ref=dst.at[slot], send_sem=send_sem.at[peer],
            recv_sem=recv_sem.at[slot], device_id=device(peer), device_id_type=MESH,
        )

    def start(d, carry):
        copy(lax.rem(me + d, owners), me).start()
        return carry

    def wait(d, carry):
        peer = lax.rem(me + d, owners)
        copy(peer, peer).wait_recv()
        copy(peer, me).wait_send()
        return carry

    return (lambda: lax.fori_loop(1, owners, start, 0)), (
        lambda: lax.fori_loop(1, owners, wait, 0)
    )


def exchange_kernel(owners, src_ref, dst_ref, send_sem, recv_sem, own_sem):
    me, device = place()
    own = pltpu.make_async_copy(src_ref, dst_ref.at[me], own_sem)
    own.start()
    greet(owners, me, device)
    start, wait = direct(owners, me, device, src_ref, dst_ref, send_sem, recv_sem)
    start()
    own.wait()
    wait()


def spread_stats(stat):
    owners = lax.axis_size(AXES)
    return pl.pallas_call(
        functools.partial(exchange_kernel, owners),
        in_specs=[pl.BlockSpec(memory_space=pl.ANY)],
        out_specs=pl.BlockSpec(memory_space=pl.ANY),
        out_shape=jax.ShapeDtypeStruct((owners,) + stat.shape, stat.dtype),
        scratch_shapes=[
            pltpu.SemaphoreType.DMA((owners,)),
            pltpu.SemaphoreType.DMA((owners,)),
            pltpu.SemaphoreType.DMA,
        ],
        compiler_params=pltpu.CompilerParams(collective_id=1, has_side_effects=True),
        name="exchange",
    )(stat)


def gather_kernel(x_ref, ids_ref, out_ref, ids_out_ref, z_send, x_send, c_send, recv, ids_send,
                  ids_recv, own_sem):
    depth, width, cores = [lax.axis_size(a) for a in AXES]
    owners = depth * width * cores
    group = lax.axis_index("groups")
    z, x, c = [lax.axis_index(a) for a in AXES]
    me, device = place()

    def slot_of(zz, xx, cc):
        return (zz * width + xx) * cores + cc

    own = pltpu.make_async_copy(x_ref, out_ref.at[me], own_sem.at[0])
    own.start()
    own_ids = pltpu.make_async_copy(ids_ref, ids_out_ref.at[me], own_sem.at[1])
    own_ids.start()
    greet(owners, me, device)

    def copy(src, slot, sem, target):
        return pltpu.make_async_remote_copy(
            src_ref=src, dst_ref=out_ref.at[slot], send_sem=sem, recv_sem=recv.at[slot],
            device_id=target, device_id_type=MESH,
        )

    def arrive(slot):
        copy(x_ref, slot, own_sem.at[0], (group, z, x, c)).wait_recv()

    def along_z(src, zz, step):
        side = 0 if step > 0 else 1
        return copy(src, slot_of(zz, x, c), z_send.at[side, zz], (group, z + step, x, c))

    def along_x(src, zz, e):
        return copy(
            src, slot_of(zz, x, c), x_send.at[e, zz], (group, z, lax.rem(x + e, width), c)
        )

    def along_c(src, zz, xx, e):
        return copy(
            src, slot_of(zz, xx, c), c_send.at[e, zz * width + xx],
            (group, z, x, lax.rem(c + e, cores)),
        )

    def spread(src, zz):
        for e in range(1, width):
            along_x(src, zz, e).start()
        for e in range(1, cores):
            along_c(src, zz, x, e).start()

    def from_x(zz):
        for e in range(1, width):
            xx = lax.rem(x + e, width)
            slot = slot_of(zz, xx, c)
            arrive(slot)
            for f in range(1, cores):
                along_c(out_ref.at[slot], zz, xx, f).start()

    @pl.when(z + 1 < depth)
    def _():
        along_z(x_ref, z, 1).start()

    @pl.when(z > 0)
    def _():
        along_z(x_ref, z, -1).start()

    spread(x_ref, z)
    start_ids, wait_ids = direct(owners, me, device, ids_ref, ids_out_ref, ids_send, ids_recv)
    start_ids()

    def step(t, carry):
        for sign in (1, -1):
            zz = z - sign * t
            known = (zz >= 0) & (zz < depth)
            onward = (z + sign >= 0) & (z + sign < depth)

            @pl.when(known)
            def _():
                slot = slot_of(zz, x, c)
                arrive(slot)

                @pl.when(onward)
                def _():
                    along_z(out_ref.at[slot], zz, sign).start()

                spread(out_ref.at[slot], zz)

        for sign in (1, -1):
            zz = z - sign * (t - 1)

            @pl.when((zz >= 0) & (zz < depth) & ((t > 1) | (sign == 1)))
            def _():
                from_x(zz)

        return carry

    lax.fori_loop(1, depth, step, 0)
    for sign in (1, -1):
        zz = z - sign * (depth - 1)

        @pl.when((zz >= 0) & (zz < depth))
        def _():
            from_x(zz)

    def last(zz, carry):
        for e in range(1, cores):
            for xx in range(width):
                arrive(slot_of(zz, xx, lax.rem(c + e, cores)))
        return carry

    lax.fori_loop(0, depth, last, 0)
    wait_ids()

    def sent(zz, carry):
        @pl.when((zz <= z) & (z + 1 < depth))
        def _():
            along_z(x_ref, zz, 1).wait_send()

        @pl.when((zz >= z) & (z > 0))
        def _():
            along_z(x_ref, zz, -1).wait_send()

        for e in range(1, width):
            along_x(x_ref, zz, e).wait_send()
        for e in range(1, cores):
            for xx in range(width):
                along_c(x_ref, zz, xx, e).wait_send()
        return carry

    lax.fori_loop(0, depth, sent, 0)
    own.wait()
    own_ids.wait()


def spread_points(points, ids):
    depth, width, cores = [lax.axis_size(a) for a in AXES]
    owners = depth * width * cores
    return pl.pallas_call(
        gather_kernel,
        in_specs=[pl.BlockSpec(memory_space=pl.ANY)] * 2,
        out_specs=[pl.BlockSpec(memory_space=pl.ANY)] * 2,
        out_shape=[
            jax.ShapeDtypeStruct((owners,) + points.shape, points.dtype),
            jax.ShapeDtypeStruct((owners,) + ids.shape, ids.dtype),
        ],
        scratch_shapes=[
            pltpu.SemaphoreType.DMA((2, depth)),
            pltpu.SemaphoreType.DMA((width, depth)),
            pltpu.SemaphoreType.DMA((cores, depth * width)),
            pltpu.SemaphoreType.DMA((owners,)),
            pltpu.SemaphoreType.DMA((owners,)),
            pltpu.SemaphoreType.DMA((owners,)),
            pltpu.SemaphoreType.DMA((2,)),
        ],
        compiler_params=pltpu.CompilerParams(collective_id=0, has_side_effects=True),
        name="gather",
    )(points, ids)


def shards(points, coarse_ids, fine_cent, slot_live, coarse_cent):
    seg, top_count = coarse_ids.shape
    blocks, slots, feature = fine_cent.shape
    owners = lax.axis_size(AXES)
    total = owners * seg
    senders = min(owners, 16)
    chunks = owners // senders
    lanes = senders * seg
    rows = senders * MOST
    inv_root = 1.0 / math.sqrt(feature)
    per = min(blocks, 4)
    steps = blocks // per
    f32, bf16 = jnp.float32, jnp.bfloat16
    params = pltpu.CompilerParams(vmem_limit_bytes=VMEM, dimension_semantics=("arbitrary",))

    ids = jnp.concatenate([coarse_ids.T] * (128 // seg), axis=1)
    all_points, all_ids = spread_points(points, ids)
    all_points = all_points.reshape(total, feature)

    key, xs = pl.pallas_call(
        functools.partial(pick_kernel, seg),
        grid=(chunks,),
        in_specs=[
            pl.BlockSpec((senders, top_count, 128), lambda i: (i, 0, 0)),
            pl.BlockSpec((lanes, feature), lambda i: (i, 0)),
        ],
        out_specs=[
            pl.BlockSpec((blocks, lanes), lambda i: (0, i)),
            pl.BlockSpec((1, blocks, rows, feature), lambda i: (i, 0, 0, 0)),
        ],
        out_shape=[
            jax.ShapeDtypeStruct((blocks, total), jnp.int32),
            jax.ShapeDtypeStruct((chunks, blocks, rows, feature), bf16),
        ],
        compiler_params=params,
        name="pick",
    )(all_ids, all_points)

    fine_spec = pl.BlockSpec((per, slots, feature), lambda i: (i, 0, 0))
    coarse_spec = pl.BlockSpec((blocks, feature), lambda i: (0, 0))
    live_spec = pl.BlockSpec((blocks, slots), lambda i: (0, 0))
    key_spec = pl.BlockSpec((blocks, total), lambda i: (0, 0))
    xs_spec = pl.BlockSpec((chunks, per, rows, feature), lambda i: (0, i, 0, 0))
    logit_spec = pl.BlockSpec((chunks, per, rows, slots), lambda i: (0, i, 0, 0))
    stat_spec = pl.BlockSpec((2, total), lambda i: (0, 0))
    all_spec = pl.BlockSpec((owners, 2, total), lambda i: (0, 0, 0))
    fine_shape = jax.ShapeDtypeStruct((blocks, slots, feature), bf16)
    logit_shape = jax.ShapeDtypeStruct((chunks, blocks, rows, slots), f32)
    stat_shape = jax.ShapeDtypeStruct((2, total), f32)
    grid_scr = pltpu.VMEM((blocks, total), f32)
    coarse_scr = pltpu.VMEM((blocks, feature), f32)
    point_scr = pltpu.VMEM((2, total), f32)

    logit, stat = pl.pallas_call(
        functools.partial(first_kernel, inv_root),
        grid=(steps,),
        in_specs=[fine_spec, coarse_spec, live_spec, key_spec, xs_spec],
        out_specs=[logit_spec, stat_spec],
        out_shape=[logit_shape, stat_shape],
        scratch_shapes=[grid_scr, grid_scr, coarse_scr],
        compiler_params=params,
        name="first",
    )(fine_cent, coarse_cent, slot_live, key, xs)
    fine = fine_cent
    for _ in range(ITERS - 1):
        every = spread_stats(stat)
        fine, logit, stat = pl.pallas_call(
            functools.partial(middle_kernel, inv_root),
            grid=(steps,),
            in_specs=[fine_spec, live_spec, key_spec, xs_spec, logit_spec, all_spec],
            out_specs=[fine_spec, logit_spec, stat_spec],
            out_shape=[fine_shape, logit_shape, stat_shape],
            scratch_shapes=[grid_scr, grid_scr, point_scr],
            compiler_params=params,
            name="middle",
        )(fine, slot_live, key, xs, logit, every)
    every = spread_stats(stat)
    fine, coarse = pl.pallas_call(
        last_kernel,
        grid=(steps,),
        in_specs=[fine_spec, live_spec, key_spec, xs_spec, logit_spec, all_spec],
        out_specs=[fine_spec, coarse_spec],
        out_shape=[fine_shape, jax.ShapeDtypeStruct((blocks, feature), bf16)],
        scratch_shapes=[point_scr, coarse_scr],
        compiler_params=params,
        name="last",
    )(fine, slot_live, key, xs, logit, every)
    return fine, coarse


def solution(mesh):
    spec = P(("groups",) + AXES)
    return jax.shard_map(
        shards, mesh=mesh, in_specs=(spec,) * 5, out_specs=(spec,) * 2, check_vma=False
    )
```

```python
import functools
import math

import jax
import jax.numpy as jnp
from jax import lax
from jax.experimental import pallas as pl
from jax.experimental.pallas import tpu as pltpu
from jax.sharding import PartitionSpec as P

MOST = 2
ITERS = 2
PRIOR = 1.0
LOW = -3.0e38
HALVES = 2
PER = 8
AXES = ("outer", "bulk", "inner")
VMEM = 56 * 1024 * 1024


def pick_kernel(seg, ids_ref, x_ref, key_ref, xs_ref):
    blocks, lanes = key_ref.shape
    rows = xs_ref.shape[2]
    block = lax.broadcasted_iota(jnp.int32, (blocks, lanes), 0)
    pos = lax.broadcasted_iota(jnp.int32, (blocks, lanes), 1)
    z, x, c = [lax.axis_index(a) for a in AXES]
    me = (z * lax.axis_size("bulk") + x) * lax.axis_size("inner") + c
    pack = 128 // seg
    part = lax.broadcasted_iota(jnp.int32, ids_ref.shape[1:], 1) // seg
    tiles = []
    for j in range(0, ids_ref.shape[0], pack):
        tile = ids_ref[j]
        for q in range(1, pack):
            tile = jnp.where(part == q, ids_ref[j + q], tile)
        tiles.append(tile)
    ids = jnp.concatenate(tiles, axis=1) - me * blocks
    member = jnp.zeros((blocks, lanes), jnp.int32)
    for k in range(ids.shape[0]):
        member = jnp.where(ids[k : k + 1, :] == block, 1, member)
    count = member
    inside = lax.rem(pos, seg)
    shift = 1
    while shift < seg:
        count = count + jnp.where(inside >= shift, pltpu.roll(count, shift, 1), 0)
        shift *= 2
    key = jnp.where(member == 1, (pos // seg) * MOST + count - member, -1)
    key_ref[...] = key
    some = 4 if lanes % (4 * seg) == 0 else lanes // seg
    tall = some * MOST
    width = some * seg
    row = lax.broadcasted_iota(jnp.int32, (tall, width), 0)
    parts = []
    for g in range(lanes // width):
        local = key[:, g * width : (g + 1) * width] - g * tall
        hot = jnp.concatenate(
            [jnp.where(local[b : b + 1, :] == row, 1.0, 0.0) for b in range(blocks)], axis=0
        ).astype(jnp.bfloat16)
        got = jnp.dot(
            hot, x_ref[g * width : (g + 1) * width, :], preferred_element_type=jnp.float32
        )
        parts.append(got.reshape(blocks, 1, tall, got.shape[1]))
    got = jnp.concatenate(parts, axis=1).reshape(blocks, rows, x_ref.shape[1])
    xs_ref[0] = got.astype(jnp.bfloat16)


def columns(rows):
    fill = jnp.zeros((128 - len(rows), 128), jnp.float32)
    turned = jnp.concatenate(list(rows) + [fill], axis=0).T
    return [jnp.broadcast_to(turned[:, b : b + 1], (128, 128)) for b in range(len(rows))]


def half_norms(squares_of):
    lane = lax.broadcasted_iota(jnp.int32, (128, 128), 1)
    wide = jnp.zeros((128, 128), jnp.float32)
    for b, square in enumerate(squares_of):
        wide = jnp.where(lane == b, 0.5 * jnp.sum(square, axis=1, keepdims=True), wide)
    turned = wide.T
    return [turned[b : b + 1, :] for b in range(len(squares_of))]


def squares(fine_ref, b):
    total = jnp.zeros((128, 128), jnp.float32)
    for j in range(0, fine_ref.shape[2], 128):
        wide = fine_ref[b, :, j : j + 128].astype(jnp.float32)
        total = total + wide * wide
    return total


def stats(fine_ref, halves, cws, lives, base, inv_root, key_ref, xs_ref, logit_ref, m_scr, s_scr):
    chunks, per, rows, width = xs_ref.shape
    lanes = key_ref.shape[1] // chunks
    row = lax.broadcasted_iota(jnp.int32, (rows, lanes), 0)
    half_c = [0.5 * jnp.sum(cw * cw, axis=1, keepdims=True) for cw in cws]
    for c in range(chunks):
        prods = [
            lax.dot_general(
                xs_ref[c, b], fine_ref[b], (((1,), (1,)), ((), ())),
                preferred_element_type=jnp.float32,
            )
            for b in range(per)
        ]
        parts = []
        for b in range(per):
            part = jnp.zeros((rows, 128), jnp.float32)
            for j in range(0, width, 128):
                wide = xs_ref[c, b, :, j : j + 128].astype(jnp.float32)
                part = part + wide * cws[b][:, j : j + 128]
            parts.append(part)
        shift = jnp.sum(jnp.concatenate(parts, axis=0), axis=1, keepdims=True)
        logits = []
        for b in range(per):
            add = (shift[b * rows : (b + 1) * rows] - half_c[b]) * inv_root
            logit = (prods[b] - halves[b]) * inv_root + add
            logits.append(jnp.where(lives[b] == 1, logit, -jnp.inf))
        logit = jnp.concatenate(logits, axis=0)
        m = jnp.max(logit, axis=1, keepdims=True)
        s = jnp.sum(jnp.exp(logit - m), axis=1, keepdims=True)
        logit_ref[c] = logit.reshape(per, rows, 128)
        part = pl.ds(c * lanes, lanes)
        tops, sums = [], []
        for b in range(per):
            hot = key_ref[pl.ds(base + b, 1), part] == row
            at = slice(b * rows, (b + 1) * rows)
            tops.append(jnp.sum(jnp.where(hot, m[at], 0.0), axis=0, keepdims=True))
            sums.append(jnp.sum(jnp.where(hot, s[at], 0.0), axis=0, keepdims=True))
        for b in range(per):
            m_scr[pl.ds(base + b, 1), part] = tops[b]
            s_scr[pl.ds(base + b, 1), part] = sums[b]


def finish(key_ref, m_scr, s_scr, stat_ref):
    has = key_ref[...] >= 0
    large = jnp.where(has, m_scr[...], LOW)
    top = jnp.max(large, axis=0, keepdims=True)
    term = s_scr[...] * jnp.exp(large - top)
    stat_ref[0:1, :] = top
    stat_ref[1:2, :] = jnp.sum(jnp.where(has, term, 0.0), axis=0, keepdims=True)


def refresh(fine_ref, new_ref, lives, base, key_ref, xs_ref, logit_ref, point_ref, norms):
    chunks, per, rows, width = xs_ref.shape
    lanes = key_ref.shape[1] // chunks
    row = lax.broadcasted_iota(jnp.int32, (rows, lanes), 0)
    mass = [jnp.full((1, 128), PRIOR, jnp.float32) for _ in range(per)]
    weights = []
    for c in range(chunks):
        part = pl.ds(c * lanes, lanes)
        tops, invs = [], []
        for b in range(per):
            hot = key_ref[pl.ds(base + b, 1), part] == row
            both = []
            for k in range(2):
                picked = jnp.where(hot, point_ref[k : k + 1, part], 0.0)
                both.append(jnp.sum(picked, axis=1, keepdims=True))
            tops.append(both[0])
            invs.append(both[1])
        inv = jnp.concatenate(invs, axis=0)
        top = jnp.where(inv > 0.0, jnp.concatenate(tops, axis=0), -LOW)
        logit = logit_ref[c].reshape(per * rows, 128)
        wide = (jnp.exp(logit - top) * inv).astype(jnp.bfloat16).astype(jnp.float32)
        turned = wide.T.astype(jnp.bfloat16)
        weights.append([turned[:, b * rows : (b + 1) * rows] for b in range(per)])
        for b in range(per):
            at = slice(b * rows, (b + 1) * rows)
            mass[b] = mass[b] + jnp.sum(wide[at], axis=0, keepdims=True)
    live_mass = [jnp.where(lives[b] == 1, mass[b], 0.0) for b in range(per)]
    both = columns([1.0 / m for m in mass] + live_mass)
    recips, shares = both[:per], both[per:]
    squares_of, coarse = [], []
    for b in range(per):
        square = jnp.zeros((128, 128), jnp.float32)
        sums = []
        for j in range(0, width, 256):
            size = min(256, width - j)
            total = jnp.zeros((128, size), jnp.float32)
            for c in range(chunks):
                total = total + jnp.dot(
                    weights[c][b], xs_ref[c, b, :, j : j + size],
                    preferred_element_type=jnp.float32,
                )
            for k in range(0, size, 128):
                at = slice(j + k, j + k + 128)
                whole = PRIOR * fine_ref[b, :, at].astype(jnp.float32) + total[:, k : k + 128]
                new = (whole * recips[b]).astype(jnp.bfloat16)
                new_ref[b, :, at] = new
                new = new.astype(jnp.float32)
                sums.append(jnp.sum(new * shares[b], axis=0, keepdims=True))
                if norms:
                    square = square + new * new
        squares_of.append(square)
        out = jnp.concatenate(sums, axis=1) / jnp.sum(live_mass[b], axis=1, keepdims=True)
        coarse.append(out.astype(jnp.bfloat16).astype(jnp.float32))
    return coarse, half_norms(squares_of) if norms else None


def rows_of(ref, base, per):
    return [ref[pl.ds(base + b, 1), :] for b in range(per)]


def first_kernel(inv_root, fine_ref, coarse_ref, live_ref, key_ref, xs_ref, logit_ref, stat_ref,
                 m_scr, s_scr, coarse_scr):
    i = pl.program_id(0)
    per = fine_ref.shape[0]
    base = i * per

    @pl.when(i == 0)
    def _():
        coarse_scr[...] = coarse_ref[...].astype(jnp.float32)

    halves = half_norms([squares(fine_ref, b) for b in range(per)])
    stats(fine_ref, halves, rows_of(coarse_scr, base, per), rows_of(live_ref, base, per), base,
          inv_root, key_ref, xs_ref, logit_ref, m_scr, s_scr)

    @pl.when(i == pl.num_programs(0) - 1)
    def _():
        finish(key_ref, m_scr, s_scr, stat_ref)


def middle_kernel(inv_root, fine_ref, live_ref, key_ref, xs_ref, logit_ref, point_ref,
                  new_ref, out_logit_ref, stat_ref, m_scr, s_scr):
    i = pl.program_id(0)
    per = fine_ref.shape[0]
    base = i * per
    lives = rows_of(live_ref, base, per)
    coarse, halves = refresh(
        fine_ref, new_ref, lives, base, key_ref, xs_ref, logit_ref, point_ref, True
    )
    stats(new_ref, halves, coarse, lives, base, inv_root, key_ref, xs_ref, out_logit_ref, m_scr,
          s_scr)

    @pl.when(i == pl.num_programs(0) - 1)
    def _():
        finish(key_ref, m_scr, s_scr, stat_ref)


def last_kernel(fine_ref, live_ref, key_ref, xs_ref, logit_ref, point_ref, new_ref, coarse_ref,
                coarse_scr):
    i = pl.program_id(0)
    per = fine_ref.shape[0]
    base = i * per
    coarse, _ = refresh(
        fine_ref, new_ref, rows_of(live_ref, base, per), base, key_ref, xs_ref, logit_ref,
        point_ref, False
    )
    for b in range(per):
        coarse_scr[pl.ds(base + b, 1), :] = coarse[b]

    @pl.when(i == pl.num_programs(0) - 1)
    def _():
        coarse_ref[...] = coarse_scr[...].astype(jnp.bfloat16)


MESH = pl.DeviceIdType.MESH


def place():
    _, width, cores = [lax.axis_size(a) for a in AXES]
    group = lax.axis_index("groups")
    z, x, c = [lax.axis_index(a) for a in AXES]

    def device(n):
        return (group, n // (width * cores), lax.rem(n // cores, width), lax.rem(n, cores))

    return (z * width + x) * cores + c, device


def greet(owners, me, device):
    barrier = pltpu.get_barrier_semaphore()

    def hello(d, carry):
        peer = lax.rem(me + d, owners)
        pl.semaphore_signal(barrier, inc=1, device_id=device(peer), device_id_type=MESH)
        return carry

    lax.fori_loop(1, owners, hello, 0)
    pl.semaphore_wait(barrier, owners - 1)


def direct(owners, me, device, src, dst, send_sem, recv_sem):
    def copy(peer, slot):
        return pltpu.make_async_remote_copy(
            src_ref=src, dst_ref=dst.at[slot], send_sem=send_sem.at[peer],
            recv_sem=recv_sem.at[slot], device_id=device(peer), device_id_type=MESH,
        )

    def start(d, carry):
        copy(lax.rem(me + d, owners), me).start()
        return carry

    def wait(d, carry):
        peer = lax.rem(me + d, owners)
        copy(peer, peer).wait_recv()
        copy(peer, me).wait_send()
        return carry

    return (lambda: lax.fori_loop(1, owners, start, 0)), (
        lambda: lax.fori_loop(1, owners, wait, 0)
    )


def exchange_kernel(owners, src_ref, point_ref, dst_ref, send_sem, recv_sem, own_sem):
    me, device = place()
    own = pltpu.make_async_copy(src_ref, dst_ref.at[me], own_sem)
    own.start()
    greet(owners, me, device)
    start, wait = direct(owners, me, device, src_ref, dst_ref, send_sem, recv_sem)
    start()
    own.wait()
    wait()
    top = dst_ref[0, 0:1, :]
    for n in range(1, owners):
        top = jnp.maximum(top, dst_ref[n, 0:1, :])
    total = jnp.zeros_like(top)
    for n in range(owners):
        total = total + dst_ref[n, 1:2, :] * jnp.exp(dst_ref[n, 0:1, :] - top)
    point_ref[0:1, :] = top
    point_ref[1:2, :] = 1.0 / total


def spread_stats(stat):
    owners = lax.axis_size(AXES)
    return pl.pallas_call(
        functools.partial(exchange_kernel, owners),
        in_specs=[pl.BlockSpec(memory_space=pltpu.VMEM)],
        out_specs=pl.BlockSpec(memory_space=pltpu.VMEM),
        out_shape=jax.ShapeDtypeStruct(stat.shape, stat.dtype),
        scratch_shapes=[
            pltpu.VMEM((owners,) + stat.shape, stat.dtype),
            pltpu.SemaphoreType.DMA((owners,)),
            pltpu.SemaphoreType.DMA((owners,)),
            pltpu.SemaphoreType.DMA,
        ],
        compiler_params=pltpu.CompilerParams(
            collective_id=1, has_side_effects=True, vmem_limit_bytes=VMEM
        ),
        name="exchange",
    )(stat)


def gather_kernel(x_ref, ids_ref, out_ref, ids_out_ref, z_send, x_send, c_send, recv, ids_send,
                  ids_recv, own_sem):
    depth, width, cores = [lax.axis_size(a) for a in AXES]
    owners = depth * width * cores
    group = lax.axis_index("groups")
    z, x, c = [lax.axis_index(a) for a in AXES]
    me, device = place()

    def slot_of(zz, xx, cc):
        return (zz * width + xx) * cores + cc

    own = pltpu.make_async_copy(x_ref, out_ref.at[me], own_sem.at[0])
    own.start()
    own_ids = pltpu.make_async_copy(ids_ref, ids_out_ref.at[me], own_sem.at[1])
    own_ids.start()
    greet(owners, me, device)

    count = recv.shape[0]
    tall = x_ref.shape[0] // count

    def part(ref, h):
        return ref.at[pl.ds(h * tall, tall)]

    def copy(src, slot, sem, h, target):
        return pltpu.make_async_remote_copy(
            src_ref=part(src, h), dst_ref=part(out_ref.at[slot], h), send_sem=sem,
            recv_sem=recv.at[h, slot], device_id=target, device_id_type=MESH,
        )

    def arrive(slot, h):
        copy(x_ref, slot, own_sem.at[0], h, (group, z, x, c)).wait_recv()

    def along_z(src, zz, step, h):
        side = 0 if step > 0 else 1
        return copy(src, slot_of(zz, x, c), z_send.at[h, side, zz], h, (group, z + step, x, c))

    def along_x(src, zz, e, h):
        return copy(
            src, slot_of(zz, x, c), x_send.at[h, e, zz], h, (group, z, lax.rem(x + e, width), c)
        )

    def along_c(src, zz, xx, e, h):
        return copy(
            src, slot_of(zz, xx, c), c_send.at[h, e, zz * width + xx], h,
            (group, z, x, lax.rem(c + e, cores)),
        )

    def spread(src, zz, h):
        for e in range(1, width):
            along_x(src, zz, e, h).start()
        for e in range(1, cores):
            along_c(src, zz, x, e, h).start()

    def from_x(zz):
        for e in range(1, width):
            xx = lax.rem(x + e, width)
            slot = slot_of(zz, xx, c)
            for h in range(count):
                arrive(slot, h)
                for f in range(1, cores):
                    along_c(out_ref.at[slot], zz, xx, f, h).start()

    for h in range(count):
        @pl.when(z + 1 < depth)
        def _():
            along_z(x_ref, z, 1, h).start()

        @pl.when(z > 0)
        def _():
            along_z(x_ref, z, -1, h).start()

        spread(x_ref, z, h)

    start_ids, wait_ids = direct(owners, me, device, ids_ref, ids_out_ref, ids_send, ids_recv)
    start_ids()

    def step(t, carry):
        for h in range(count):
            for sign in (1, -1):
                zz = z - sign * t
                known = (zz >= 0) & (zz < depth)
                onward = (z + sign >= 0) & (z + sign < depth)

                @pl.when(known)
                def _():
                    slot = slot_of(zz, x, c)
                    arrive(slot, h)

                    @pl.when(onward)
                    def _():
                        along_z(out_ref.at[slot], zz, sign, h).start()

                    spread(out_ref.at[slot], zz, h)

        for sign in (1, -1):
            zz = z - sign * (t - 1)

            @pl.when((zz >= 0) & (zz < depth) & ((t > 1) | (sign == 1)))
            def _():
                from_x(zz)

        return carry

    lax.fori_loop(1, depth, step, 0)
    for sign in (1, -1):
        zz = z - sign * (depth - 1)

        @pl.when((zz >= 0) & (zz < depth))
        def _():
            from_x(zz)

    def last(zz, carry):
        for h in range(count):
            for e in range(1, cores):
                for xx in range(width):
                    arrive(slot_of(zz, xx, lax.rem(c + e, cores)), h)
        return carry

    lax.fori_loop(0, depth, last, 0)
    wait_ids()

    def sent(zz, carry):
        for h in range(count):
            @pl.when((zz <= z) & (z + 1 < depth))
            def _():
                along_z(x_ref, zz, 1, h).wait_send()

            @pl.when((zz >= z) & (z > 0))
            def _():
                along_z(x_ref, zz, -1, h).wait_send()

            for e in range(1, width):
                along_x(x_ref, zz, e, h).wait_send()
            for e in range(1, cores):
                for xx in range(width):
                    along_c(x_ref, zz, xx, e, h).wait_send()
        return carry

    lax.fori_loop(0, depth, sent, 0)
    own.wait()
    own_ids.wait()


def spread_points(points, ids):
    depth, width, cores = [lax.axis_size(a) for a in AXES]
    owners = depth * width * cores
    return pl.pallas_call(
        gather_kernel,
        in_specs=[pl.BlockSpec(memory_space=pl.ANY)] * 2,
        out_specs=[pl.BlockSpec(memory_space=pl.ANY)] * 2,
        out_shape=[
            jax.ShapeDtypeStruct((owners,) + points.shape, points.dtype),
            jax.ShapeDtypeStruct((owners,) + ids.shape, ids.dtype),
        ],
        scratch_shapes=[
            pltpu.SemaphoreType.DMA((HALVES, 2, depth)),
            pltpu.SemaphoreType.DMA((HALVES, width, depth)),
            pltpu.SemaphoreType.DMA((HALVES, cores, depth * width)),
            pltpu.SemaphoreType.DMA((HALVES, owners)),
            pltpu.SemaphoreType.DMA((owners,)),
            pltpu.SemaphoreType.DMA((owners,)),
            pltpu.SemaphoreType.DMA((2,)),
        ],
        compiler_params=pltpu.CompilerParams(collective_id=0, has_side_effects=True),
        name="gather",
    )(points, ids)


def shards(points, coarse_ids, fine_cent, slot_live, coarse_cent):
    seg, top_count = coarse_ids.shape
    blocks, slots, feature = fine_cent.shape
    owners = lax.axis_size(AXES)
    total = owners * seg
    senders = min(owners, 16)
    chunks = owners // senders
    lanes = senders * seg
    rows = senders * MOST
    inv_root = 1.0 / math.sqrt(feature)
    per = min(blocks, PER)
    steps = blocks // per
    f32, bf16 = jnp.float32, jnp.bfloat16
    params = pltpu.CompilerParams(vmem_limit_bytes=VMEM, dimension_semantics=("arbitrary",))

    ids = jnp.concatenate([coarse_ids.T] * (128 // seg), axis=1)
    all_points, all_ids = spread_points(points, ids)
    all_points = all_points.reshape(total, feature)

    key, xs = pl.pallas_call(
        functools.partial(pick_kernel, seg),
        grid=(chunks,),
        in_specs=[
            pl.BlockSpec((senders, top_count, 128), lambda i: (i, 0, 0)),
            pl.BlockSpec((lanes, feature), lambda i: (i, 0)),
        ],
        out_specs=[
            pl.BlockSpec((blocks, lanes), lambda i: (0, i)),
            pl.BlockSpec((1, blocks, rows, feature), lambda i: (i, 0, 0, 0)),
        ],
        out_shape=[
            jax.ShapeDtypeStruct((blocks, total), jnp.int32),
            jax.ShapeDtypeStruct((chunks, blocks, rows, feature), bf16),
        ],
        compiler_params=params,
        name="pick",
    )(all_ids, all_points)

    fine_spec = pl.BlockSpec((per, slots, feature), lambda i: (i, 0, 0))
    coarse_spec = pl.BlockSpec((blocks, feature), lambda i: (0, 0))
    live_spec = pl.BlockSpec((blocks, slots), lambda i: (0, 0))
    key_spec = pl.BlockSpec((blocks, total), lambda i: (0, 0))
    xs_spec = pl.BlockSpec((chunks, per, rows, feature), lambda i: (0, i, 0, 0))
    logit_spec = pl.BlockSpec((chunks, per, rows, slots), lambda i: (0, i, 0, 0))
    stat_spec = pl.BlockSpec((2, total), lambda i: (0, 0))
    fine_shape = jax.ShapeDtypeStruct((blocks, slots, feature), bf16)
    logit_shape = jax.ShapeDtypeStruct((chunks, blocks, rows, slots), f32)
    stat_shape = jax.ShapeDtypeStruct((2, total), f32)
    grid_scr = pltpu.VMEM((blocks, total), f32)
    coarse_scr = pltpu.VMEM((blocks, feature), f32)

    logit, stat = pl.pallas_call(
        functools.partial(first_kernel, inv_root),
        grid=(steps,),
        in_specs=[fine_spec, coarse_spec, live_spec, key_spec, xs_spec],
        out_specs=[logit_spec, stat_spec],
        out_shape=[logit_shape, stat_shape],
        scratch_shapes=[grid_scr, grid_scr, coarse_scr],
        compiler_params=params,
        name="first",
    )(fine_cent, coarse_cent, slot_live, key, xs)
    fine = fine_cent
    for _ in range(ITERS - 1):
        every = spread_stats(stat)
        fine, logit, stat = pl.pallas_call(
            functools.partial(middle_kernel, inv_root),
            grid=(steps,),
            in_specs=[fine_spec, live_spec, key_spec, xs_spec, logit_spec, stat_spec],
            out_specs=[fine_spec, logit_spec, stat_spec],
            out_shape=[fine_shape, logit_shape, stat_shape],
            scratch_shapes=[grid_scr, grid_scr],
            compiler_params=params,
            name="middle",
        )(fine, slot_live, key, xs, logit, every)
    every = spread_stats(stat)
    fine, coarse = pl.pallas_call(
        last_kernel,
        grid=(steps,),
        in_specs=[fine_spec, live_spec, key_spec, xs_spec, logit_spec, stat_spec],
        out_specs=[fine_spec, coarse_spec],
        out_shape=[fine_shape, jax.ShapeDtypeStruct((blocks, feature), bf16)],
        scratch_shapes=[coarse_scr],
        compiler_params=params,
        name="last",
    )(fine, slot_live, key, xs, logit, every)
    return fine, coarse


def solution(mesh):
    spec = P(("groups",) + AXES)
    return jax.shard_map(
        shards, mesh=mesh, in_specs=(spec,) * 5, out_specs=(spec,) * 2, check_vma=False
    )
```
